32 devices in a mesh: dp: 2 (over x), expert: 16 (over z, y, core).
Axes of the slice: x: 2, y: 2, z: 4, core: 2. Of those that a mesh axis runs over, the one named last changes fastest.
Arguments:
- tokens: bfloat16 [128, 4096], P(('dp', 'expert')), may hold values from -6 to 6
- grad_output: bfloat16 [128, 4096], P(('dp', 'expert')), may hold values from -6 to 6
- routes: int32 [128, 8], P(('dp', 'expert')), may hold values from 0 to 15, all different within a row; in each aligned block of 4 rows (0 to 3, 4 to 7, ...) at most 3 rows name the same one
- gate_weights: float32 [128, 8], P(('dp', 'expert')), may hold values from 0.05 to 1
- gate_proj: bfloat16 [16, 1536, 4096], P('expert', 'dp'), may hold values from -0.09375 to 0.09375
- up_proj: bfloat16 [16, 1536, 4096], P('expert', 'dp'), may hold values from -0.09375 to 0.09375
- down_proj: bfloat16 [16, 1536, 4096], P('expert', 'dp'), may hold values from -0.15625 to 0.15625
Outputs:
- layer_out: bfloat16 [128, 4096], P(('dp', 'expert'))
- grad_tokens: bfloat16 [128, 4096], P(('dp', 'expert'))
- grad_gates: float32 [128, 8], P(('dp', 'expert'))
- grad_gate_proj: bfloat16 [16, 1536, 4096], P('expert', 'dp')
- grad_up_proj: bfloat16 [16, 1536, 4096], P('expert', 'dp')
- grad_down_proj: bfloat16 [16, 1536, 4096], P('expert', 'dp')
The draws below stay inside these ranges and needn't reach their ends.
Inputs may be any that keep to these rules, and one draw needn't show every extreme that they name: `routes`: each row names 8 different experts. Among the 4 tokens of one device no expert is named by more than 3 tokens, a bound that some block reaches.
All inputs are finite; a program needn't handle non-finite values.
Results may differ from the reference program's by a relative error of at most 0.0095.
Values may be sent and summed in bfloat16 or wider, within the bound.
A program may use at most 128 MiB of HBM per device.

```python
import math
import jax
import jax.numpy as jnp
import numpy as np
from jax import lax

D = 4096
FF = 1536
TOPK = 8
TOK_DEV = 4
EXPERTS = 16
TOKENS = 128
CAP = 3
N_DP = 2
N_EXPERT = 16


def shard_levels(key, dims, shards, least, largest):
    gain, own = 1.0, jax.random.fold_in(key, 6)
    for dim, blocks in shards:
        draws = jnp.exp(jax.random.uniform(jax.random.fold_in(own, dim), (blocks,), jnp.float32, least / len(shards), largest / len(shards)))
        gain = gain * jnp.repeat(draws, dims[dim] // blocks).reshape([-1 if axis == dim else 1 for axis in range(len(dims))])
    return gain


def routed_block(rng, own, number, rows, number_of, top, limit, skew):
    ranking = jax.random.permutation(rng, number_of)
    packed, ordinary = shares(number_of, rows * top, limit, skew, True), shares(number_of, rows * top, limit, skew, False)
    places = jnp.arange(number_of)

    def named(sizes, turn):
        used = int((sizes > 0).sum())
        fixed = max(1, used // 4)
        passed = fixed + (places - fixed + turn * (used - fixed)) % max(1, number_of - fixed)
        return jnp.zeros((number_of,), jnp.int32).at[ranking[jnp.where(places < fixed, places, passed)]].set(jnp.asarray(sizes, jnp.int32))

    sizes = jnp.where(number % 4 == 0, named(packed, number // 4), named(ordinary, number - number // 4 - 1))
    mixed = jax.random.permutation(jax.random.fold_in(own, 3), number_of)
    donor, sink = mixed[0:number_of // 2 * 2:2], mixed[1:number_of // 2 * 2:2]
    margin = jnp.minimum(sizes[donor] - 1, limit - sizes[sink]) // 2
    margin = jnp.where((donor == ranking[0]) | (sink == ranking[0]) | (sizes[sink] == 0), 0, jnp.maximum(margin, 0))
    passed = jax.random.randint(jax.random.fold_in(own, 4), (number_of // 2,), 0, 1 << 20) % (margin + 1)
    sizes = sizes.at[donor].add(-passed).at[sink].add(passed)
    items = jnp.searchsorted(jnp.cumsum(sizes), jnp.arange(rows * top), side="right").astype(jnp.int32)
    table = items.reshape(top, rows).T
    table = table[jax.random.permutation(jax.random.fold_in(own, 1), rows)]
    turn = jax.random.randint(jax.random.fold_in(own, 2), (rows, 1), 0, top)
    return jnp.take_along_axis(table, (jnp.arange(top)[None, :] + turn) % top, axis=1)


def shares(count, total, bound, skew, full):
    loads = [(1 << 20) // math.isqrt(standing ** skew) + 1 for standing in range(1, count + 1)]
    largest = bound if full else min(bound, max(-(-total // count), total * loads[0] // sum(loads)))
    least = 1 if total - largest >= count - 1 else 0
    counts, rest = [largest] + [least] * (count - 1), total - largest - least * (count - 1)
    while rest > 0:
        movable = [i for i in range(1, count) if counts[i] < largest] or [i for i in range(1, count) if counts[i] < bound]
        whole, budget = sum([loads[i] for i in movable]), rest
        for i in movable:
            addition = min(bound - counts[i], max(1, budget * loads[i] // whole), rest)
            counts[i] = counts[i] + addition
            rest = rest - addition
    return np.array(counts)


def scatter_about(key, dims, width, most, split=(), kind=jnp.bfloat16):
    entries = jax.random.normal(key, dims, jnp.float32) * width
    if len(split) > 0:
        entries = shard_levels(key, dims, split, -0.22, 0.18) * entries
    return jnp.clip(entries, min=-most, max=most).astype(kind)


def setup_inputs(seed: int = 0) -> dict:
    key_list = jax.random.split(jax.random.key(seed), 8)
    tokens = scatter_about(key_list[0], (TOKENS, D), 1.0, 6.0, ((0, 32),))
    grad_output = scatter_about(key_list[1], (TOKENS, D), 1.0, 6.0, ((0, 32),))
    routes_keys = jax.random.split(jax.random.fold_in(key_list[2], 1), TOKENS // TOK_DEV)
    routes_turns = jax.random.permutation(jax.random.fold_in(key_list[2], 3), TOKENS // TOK_DEV)
    routes = jax.vmap(lambda own, number: routed_block(jax.random.fold_in(key_list[2], 2), own, number, TOK_DEV, EXPERTS, TOPK, CAP, 2))(routes_keys, routes_turns).reshape((TOKENS, TOPK))
    gate_weights = jnp.clip(jnp.exp(math.log(1.0) - 2.9957323 * jax.random.uniform(key_list[3], (TOKENS, TOPK), jnp.float32) ** shard_levels(key_list[3], (TOKENS, TOPK), ((0, 32),), -0.2, 0.2)), 0.05, 1.0)
    gate_proj = scatter_about(key_list[4], (EXPERTS, FF, D), D ** -0.5, 0.09375, ((0, 16), (1, 2)))
    up_proj = scatter_about(key_list[5], (EXPERTS, FF, D), D ** -0.5, 0.09375, ((0, 16), (1, 2)))
    down_proj = scatter_about(key_list[6], (EXPERTS, FF, D), FF ** -0.5, 0.15625, ((0, 16), (1, 2)))
    return dict(tokens=tokens, grad_output=grad_output, routes=routes, gate_weights=gate_weights, gate_proj=gate_proj, up_proj=up_proj, down_proj=down_proj)


def silu_parts(pre_act):
    squash = jax.nn.sigmoid(pre_act)
    return pre_act * squash, squash * (1.0 + pre_act * (1.0 - squash))


def contract_last(left, right):
    return lax.dot_general(left, right, (((1,), (1,)), ((), ())), preferred_element_type=jnp.float32)


def contract_first(left, right):
    return lax.dot_general(left, right, (((0,), (0,)), ((), ())), preferred_element_type=jnp.float32)


def expert_rows(x_rows, g_rows, gate_part, up_part, down_part):
    pre_gate = contract_last(x_rows, gate_part)
    pre_up = contract_last(x_rows, up_part)
    active, slope_term = silu_parts(pre_gate)
    hidden = (active * pre_up).astype(jnp.bfloat16)
    out_part = jnp.dot(hidden, down_part, preferred_element_type=jnp.float32).astype(jnp.bfloat16)
    d_hidden = contract_last(g_rows, down_part)
    d_upper = (d_hidden * active).astype(jnp.bfloat16)
    d_lower = (d_hidden * pre_up * slope_term).astype(jnp.bfloat16)
    back_part = (jnp.dot(d_lower, gate_part, preferred_element_type=jnp.float32)
                 + jnp.dot(d_upper, up_part, preferred_element_type=jnp.float32)).astype(jnp.bfloat16)
    grad_list = (contract_first(d_lower, x_rows), contract_first(d_upper, x_rows), contract_first(hidden, g_rows))
    return out_part, back_part, grad_list


def reference(tokens, grad_output, routes, gate_weights, gate_proj, up_proj, down_proj):
    count_rows = min(TOKENS, CAP * N_DP * N_EXPERT)
    block_width = FF // N_DP
    flat_ids = routes.reshape(-1)
    flat_gate = gate_weights.reshape(-1)

    def one_expert(state_carry, expert):
        out_acc, back_acc, gate_acc = state_carry
        is_routed = flat_ids == expert
        positions = jnp.nonzero(is_routed, size=count_rows, fill_value=0)[0].astype(jnp.int32)
        is_valid = jnp.arange(count_rows, dtype=jnp.int32) < jnp.sum(is_routed.astype(jnp.int32))
        token_idx = (positions // TOPK).astype(jnp.int32)
        x_rows = jnp.where(is_valid[:, None], tokens[token_idx], jnp.zeros((), jnp.bfloat16))
        dy_rows = grad_output[token_idx]
        row_gate = jnp.where(is_valid, flat_gate[positions], jnp.zeros((), jnp.float32))
        g_rows = (row_gate[:, None] * dy_rows.astype(jnp.float32)).astype(jnp.bfloat16)
        gate_full = gate_proj[expert]
        up_full = up_proj[expert]
        down_full = down_proj[expert]
        out_sum = jnp.zeros((count_rows, D), jnp.float32)
        back_sum = jnp.zeros((count_rows, D), jnp.float32)
        gate_blocks = []
        up_blocks = []
        down_blocks = []
        for block_idx in range(N_DP):
            low = block_idx * block_width
            high = low + block_width
            out_part, back_part, grad_list = expert_rows(x_rows, g_rows, gate_full[low:high, :], up_full[low:high, :], down_full[low:high, :])
            out_sum = out_sum + out_part.astype(jnp.float32)
            back_sum = back_sum + back_part.astype(jnp.float32)
            gate_blocks.append(grad_list[0])
            up_blocks.append(grad_list[1])
            down_blocks.append(grad_list[2])
        out_acc = out_acc.at[token_idx].add(row_gate[:, None] * out_sum)
        back_acc = back_acc.at[token_idx].add(jnp.where(is_valid[:, None], back_sum, jnp.zeros((), jnp.float32)))
        inner_prods = jnp.sum(dy_rows.astype(jnp.float32) * out_sum, axis=1)
        gate_acc = gate_acc.at[positions].add(jnp.where(is_valid, inner_prods, jnp.zeros((), jnp.float32)))
        grads_out = (jnp.concatenate(gate_blocks, axis=0).astype(jnp.bfloat16),
                     jnp.concatenate(up_blocks, axis=0).astype(jnp.bfloat16),
                     jnp.concatenate(down_blocks, axis=0).astype(jnp.bfloat16))
        return (out_acc, back_acc, gate_acc), grads_out

    start_state = (jnp.zeros((TOKENS, D), jnp.float32), jnp.zeros((TOKENS, D), jnp.float32),
                   jnp.zeros((TOKENS * TOPK,), jnp.float32))
    final_state, grads_all = lax.scan(one_expert, start_state, jnp.arange(EXPERTS, dtype=jnp.int32))
    out_acc, back_acc, gate_acc = final_state
    return (out_acc.astype(jnp.bfloat16), back_acc.astype(jnp.bfloat16), gate_acc.reshape(TOKENS, TOPK),
            grads_all[0], grads_all[1], grads_all[2])
```

```python
import functools

import jax
import jax.numpy as jnp
from jax import lax
from jax.experimental import pallas as pl
from jax.experimental.pallas import tpu as pltpu
from jax.sharding import PartitionSpec as P

MESH = pl.DeviceIdType.MESH
LANES = 128
VMEM_BYTES = 56 * 1024 * 1024


def contract_last(left, right):
    return lax.dot_general(
        left, right, (((1,), (1,)), ((), ())), preferred_element_type=jnp.float32
    )


def contract_first(left, right):
    return lax.dot_general(
        left, right, (((0,), (0,)), ((), ())), preferred_element_type=jnp.float32
    )


class Place:
    def __init__(self, groups, hi):
        self.groups, self.hi = groups, hi
        self.d = lax.axis_index("dp")
        e = lax.axis_index("expert")
        self.z, self.u, self.v = e // 4, (e // 2) % 2, e % 2

    def at(self, d=None, z=None, u=None, v=None):
        d = self.d if d is None else d
        z = self.z if z is None else z
        u = self.u if u is None else u
        v = self.v if v is None else v
        return (d, (z * 2 + u) * 2 + v)

    def peers(self):
        found = [self.at(z=(self.z + k) % self.hi) for k in range(1, self.hi)]
        found += [self.at(d=(self.d + k) % self.groups) for k in range(1, self.groups)]
        return found + [self.at(u=1 - self.u), self.at(v=1 - self.v)]


def greet(place):
    barrier = pltpu.get_barrier_semaphore()
    peers = place.peers()
    for peer in peers:
        pl.semaphore_signal(barrier, inc=1, device_id=peer, device_id_type=MESH)
    pl.semaphore_wait(barrier, len(peers))


class Sender:
    def __init__(self, send, recv):
        self.send, self.recv, self.used = send, recv, 0

    def start(self, src, dst, peer):
        slot = self.used
        self.used += 1
        copy = pltpu.make_async_remote_copy(
            src_ref=src,
            dst_ref=dst,
            send_sem=self.send.at[slot],
            recv_sem=self.recv.at[slot],
            device_id=peer,
            device_id_type=MESH,
        )
        copy.start()
        return copy


def gather_kernel(groups, hi, x_ref, y_ref, m_ref, xo, yo, mo, send, recv, local):
    p = Place(groups, hi)
    d, z, u, v = p.d, p.z, p.u, p.v
    greet(p)
    sender = Sender(send, recv)
    trio = ((x_ref, xo), (m_ref, mo), (y_ref, yo))
    first = []
    for k in range(1, hi):
        for src, out in trio:
            first.append(sender.start(src, out.at[v, u, d, z], p.at(z=(z + k) % hi)))
    own = []
    for i, (src, out) in enumerate(trio):
        copy = pltpu.make_async_copy(src, out.at[v, u, d, z], local.at[i])
        copy.start()
        own.append(copy)
    for copy in own:
        copy.wait()
    for copy in first:
        copy.wait_recv()
    second, last = [], []
    for out in (xo, mo):
        block = out.at[v, u, d]
        for k in range(1, groups):
            second.append(sender.start(block, block, p.at(d=(d + k) % groups)))
    block = yo.at[v, u, d]
    second.append(sender.start(block, block, p.at(u=1 - u)))
    for _, out in trio:
        block = out.at[v, u, d]
        last.append(sender.start(block, block, p.at(v=1 - v)))
    for copy in second:
        copy.wait_recv()
    third = []
    for out in (xo, mo):
        block = out.at[v, u]
        third.append(sender.start(block, block, p.at(u=1 - u)))
    block = yo.at[v, :, d]
    for k in range(1, groups):
        third.append(sender.start(block, block, p.at(d=(d + k) % groups)))
    for out in (xo, mo):
        for k in range(1, groups):
            block = out.at[v, u, (d + k) % groups]
            last.append(sender.start(block, block, p.at(v=1 - v)))
    block = yo.at[v, 1 - u, d]
    last.append(sender.start(block, block, p.at(v=1 - v)))
    for copy in third:
        copy.wait_recv()
    for out in (xo, mo):
        block = out.at[v, 1 - u]
        last.append(sender.start(block, block, p.at(v=1 - v)))
    for k in range(1, groups):
        block = yo.at[v, :, (d + k) % groups]
        last.append(sender.start(block, block, p.at(v=1 - v)))
    for copy in last:
        copy.wait_recv()
    for copy in first + second + third + last:
        copy.wait_send()


def gather_all(groups, hi, x, y, m):
    shape = (2, 2, groups, hi)
    copies = 3 * (hi - 1) + 2 * (2 * (groups - 1)) + 2 * (groups - 1) + 3 * 4 + 8
    vmem = pl.BlockSpec(memory_space=pltpu.VMEM)
    return pl.pallas_call(
        functools.partial(gather_kernel, groups, hi),
        out_shape=[jax.ShapeDtypeStruct(shape + a.shape, a.dtype) for a in (x, y, m)],
        in_specs=[vmem] * 3,
        out_specs=[vmem] * 3,
        scratch_shapes=[
            pltpu.SemaphoreType.DMA((copies,)),
            pltpu.SemaphoreType.DMA((copies,)),
            pltpu.SemaphoreType.DMA((3,)),
        ],
        compiler_params=pltpu.CompilerParams(
            collective_id=0, has_side_effects=True, vmem_limit_bytes=VMEM_BYTES
        ),
        name="gather_all",
    )(x, y, m)


def add_into(dst, terms, lead):
    total = 1
    for n in lead:
        total *= n

    def step(i, carry):
        index, rest = [], i
        for n in reversed(lead):
            index.insert(0, rest % n)
            rest = rest // n
        acc = terms[0][tuple(index)].astype(jnp.float32)
        for term in terms[1:]:
            acc = acc + term[tuple(index)].astype(jnp.float32)
        dst[tuple(index)] = acc.astype(dst.dtype)
        return carry

    lax.fori_loop(0, total, step, 0)


def scatter_kernel(groups, hi, *refs):
    ins, outs = refs[0:3], refs[3:6]
    work = [refs[6 + 7 * i : 13 + 7 * i] for i in range(3)]
    send, recv = refs[27:29]
    p = Place(groups, hi)
    d, z, u, v = p.d, p.z, p.u, p.v
    greet(p)
    sender = Sender(send, recv)
    copies = []
    stage1 = []
    for part, (r1, *_) in zip(ins, work):
        stage1.append(sender.start(part.at[1 - v], r1, p.at(v=1 - v)))
    stage2 = []
    for i, (part, (r1, s1, r2, *_)) in enumerate(zip(ins, work)):
        stage1[i].wait_recv()
        add_into(s1, (part.at[v], r1), (2, groups, hi))
        if i == 1:
            stage2.append(
                [
                    sender.start(s1.at[:, (d + k) % groups], r2.at[k - 1], p.at(d=(d + k) % groups))
                    for k in range(1, groups)
                ]
            )
        else:
            stage2.append([sender.start(s1.at[1 - u], r2, p.at(u=1 - u))])
    stage3 = []
    for i, (r1, s1, r2, s2, r3, s3, r4) in enumerate(work):
        for copy in stage2[i]:
            copy.wait_recv()
        if i == 1:
            terms = [s1.at[:, d]] + [r2.at[k - 1] for k in range(1, groups)]
            add_into(s2, terms, (2, hi))
            stage3.append([sender.start(s2.at[1 - u], r3, p.at(u=1 - u))])
        else:
            add_into(s2, (s1.at[u], r2), (groups, hi))
            stage3.append(
                [
                    sender.start(s2.at[(d + k) % groups], r3.at[k - 1], p.at(d=(d + k) % groups))
                    for k in range(1, groups)
                ]
            )
    stage4 = []
    for i, (r1, s1, r2, s2, r3, s3, r4) in enumerate(work):
        for copy in stage3[i]:
            copy.wait_recv()
        if i == 1:
            add_into(s3, (s2.at[u], r3), (hi,))
        else:
            add_into(s3, [s2.at[d]] + [r3.at[k - 1] for k in range(1, groups)], (hi,))
        stage4.append(
            [
                sender.start(s3.at[(z + k) % hi], r4.at[k - 1], p.at(z=(z + k) % hi))
                for k in range(1, hi)
            ]
        )
    for i, (r1, s1, r2, s2, r3, s3, r4) in enumerate(work):
        for copy in stage4[i]:
            copy.wait_recv()
        acc = s3[z].astype(jnp.float32)
        for k in range(1, hi):
            acc = acc + r4[k - 1].astype(jnp.float32)
        outs[i][...] = acc.astype(outs[i].dtype)
    for copy in stage1 + sum(stage2 + stage3 + stage4, []):
        copy.wait_send()


def scatter_all(groups, hi, parts):
    scratch = []
    for i, part in enumerate(parts):
        tail = part.shape[4:]
        by_u = i != 1
        shapes = [
            (2, groups, hi),
            (2, groups, hi),
            (groups, hi) if by_u else (groups - 1, 2, hi),
            (groups, hi) if by_u else (2, hi),
            (groups - 1, hi) if by_u else (hi,),
            (hi,),
            (hi - 1,),
        ]
        scratch += [pltpu.VMEM(s + tail, part.dtype) for s in shapes]
    copies = 3 * (groups + 1 + hi)
    vmem = pl.BlockSpec(memory_space=pltpu.VMEM)
    return pl.pallas_call(
        functools.partial(scatter_kernel, groups, hi),
        out_shape=[jax.ShapeDtypeStruct(a.shape[4:], a.dtype) for a in parts],
        in_specs=[vmem] * 3,
        out_specs=[vmem] * 3,
        scratch_shapes=scratch
        + [pltpu.SemaphoreType.DMA((copies,)), pltpu.SemaphoreType.DMA((copies,))],
        compiler_params=pltpu.CompilerParams(
            collective_id=1, has_side_effects=True, vmem_limit_bytes=VMEM_BYTES
        ),
        name="scatter_all",
    )(*parts)


def body(tokens, grad_output, routes, gate_weights, gate_proj, up_proj, down_proj):
    experts = lax.axis_size("expert")
    groups = lax.axis_size("dp")
    hi = experts // 4
    token_count, feature_dim = tokens.shape
    me = lax.axis_index("expert")
    gate_local, up_local, down_local = gate_proj[0], up_proj[0], down_proj[0]
    lanes = jnp.arange(LANES, dtype=jnp.int32)
    chosen = routes[:, :, None] == lanes[None, None, :]
    dense = jnp.sum(jnp.where(chosen, gate_weights[:, :, None], 0.0), axis=1)
    x_all, dy_all, dense_all = gather_all(groups, hi, tokens, grad_output, dense)
    lead = x_all.shape[:5]
    x_rows = x_all.reshape(-1, feature_dim)
    dy_rows = dy_all.reshape(-1, feature_dim)
    mine = (lanes == me)[None, :]
    gate = jnp.sum(jnp.where(mine, dense_all.reshape(-1, LANES), 0.0), axis=1, keepdims=True)

    pre_gate = contract_last(x_rows, gate_local)
    pre_up = contract_last(x_rows, up_local)
    raw = contract_last(dy_rows, down_local)
    squash = jax.nn.sigmoid(pre_gate)
    active = pre_gate * squash
    slope = squash * (1.0 + pre_gate * (1.0 - squash))
    hidden = active * pre_up
    inner = jnp.sum(hidden * raw, axis=1, keepdims=True)
    hidden_g = (gate * hidden).astype(jnp.bfloat16)
    d_hidden = gate * raw
    d_upper = (d_hidden * active).astype(jnp.bfloat16)
    d_lower = (d_hidden * pre_up * slope).astype(jnp.bfloat16)
    out_part = jnp.dot(hidden_g, down_local, preferred_element_type=jnp.float32)
    back_part = jnp.dot(d_lower, gate_local, preferred_element_type=jnp.float32) + jnp.dot(
        d_upper, up_local, preferred_element_type=jnp.float32
    )
    inner_part = jnp.where(mine, inner, 0.0)
    layer_out, grad_tokens, inner_sum = scatter_all(
        groups,
        hi,
        (
            out_part.astype(jnp.bfloat16).reshape(lead + (feature_dim,)),
            back_part.astype(jnp.bfloat16).reshape(lead + (feature_dim,)),
            inner_part.reshape(lead + (LANES,)),
        ),
    )
    grad_gates = jnp.sum(jnp.where(chosen, inner_sum[:, None, :], 0.0), axis=2)
    return (
        layer_out,
        grad_tokens,
        grad_gates,
        contract_first(d_lower, x_rows).astype(jnp.bfloat16)[None],
        contract_first(d_upper, x_rows).astype(jnp.bfloat16)[None],
        contract_first(hidden_g, dy_rows).astype(jnp.bfloat16)[None],
    )


def solution(mesh):
    row = P(("dp", "expert"), None)
    weight = P("expert", "dp", None)
    return jax.shard_map(
        body,
        mesh=mesh,
        in_specs=(row,) * 4 + (weight,) * 3,
        out_specs=(row,) * 3 + (weight,) * 3,
        check_vma=False,
    )
```

```python
import functools

import jax
import jax.numpy as jnp
from jax import lax
from jax.experimental import pallas as pl
from jax.experimental.pallas import tpu as pltpu
from jax.sharding import PartitionSpec as P

MESH = pl.DeviceIdType.MESH
LANES = 128
UNIT = 8
CHUNKS = 4
VMEM_BYTES = 62 * 1024 * 1024


class Place:
    def __init__(self, groups, hi):
        self.groups, self.hi = groups, hi
        self.d = lax.axis_index("dp")
        e = lax.axis_index("expert")
        self.z, self.u, self.v = e // 4, (e // 2) % 2, e % 2

    def at(self, d=None, z=None, u=None, v=None):
        d = self.d if d is None else d
        z = self.z if z is None else z
        u = self.u if u is None else u
        v = self.v if v is None else v
        return (d, (z * 2 + u) * 2 + v)

    def peers(self):
        found = [self.at(z=(self.z + k) % self.hi) for k in range(1, self.hi)]
        found += [self.at(d=(self.d + k) % self.groups) for k in range(1, self.groups)]
        return found + [self.at(u=1 - self.u), self.at(v=1 - self.v)]


def greet(place):
    barrier = pltpu.get_barrier_semaphore()
    peers = place.peers()
    for peer in peers:
        pl.semaphore_signal(barrier, inc=1, device_id=peer, device_id_type=MESH)
    pl.semaphore_wait(barrier, len(peers))


class Sender:
    def __init__(self, send, recv):
        self.send, self.recv, self.used = send, recv, 0

    def start(self, src, dst, peer):
        slot = self.used
        self.used += 1
        copy = pltpu.make_async_remote_copy(
            src_ref=src,
            dst_ref=dst,
            send_sem=self.send.at[slot],
            recv_sem=self.recv.at[slot],
            device_id=peer,
            device_id_type=MESH,
        )
        copy.start()
        return copy


def wait_all(copies):
    for copy in copies:
        copy.wait_recv()


def gather(p, sender, sources):
    groups, hi = p.groups, p.hi
    d, z, u, v = p.d, p.z, p.u, p.v
    every = []

    def send(src, dst, peer):
        copy = sender.start(src, dst, peer)
        every.append(copy)
        return copy

    first = []
    for src, out, cols, _ in sources:
        first.append(
            [
                send(src.at[:, cols], out.at[v, u, d, z, :, cols], p.at(z=(z + k) % hi))
                for k in range(1, hi)
            ]
        )
    yield None
    second, third, last = [], [], []
    for i, (_, out, cols, u_first) in enumerate(sources):
        wait_all(first[i])
        block = out.at[v, u, d, :, :, cols]
        if u_first:
            second.append([send(block, block, p.at(u=1 - u))])
        else:
            second.append([send(block, block, p.at(d=(d + k) % groups)) for k in range(1, groups)])
        last.append(send(block, block, p.at(v=1 - v)))
    for i, (_, out, cols, u_first) in enumerate(sources):
        wait_all(second[i])
        if u_first:
            block = out.at[v, :, d, :, :, cols]
            third.append([send(block, block, p.at(d=(d + k) % groups)) for k in range(1, groups)])
            block = out.at[v, 1 - u, d, :, :, cols]
            last.append(send(block, block, p.at(v=1 - v)))
        else:
            block = out.at[v, u, :, :, :, cols]
            third.append([send(block, block, p.at(u=1 - u))])
            for k in range(1, groups):
                block = out.at[v, u, (d + k) % groups, :, :, cols]
                last.append(send(block, block, p.at(v=1 - v)))
    for i, (_, out, cols, u_first) in enumerate(sources):
        wait_all(third[i])
        if u_first:
            for k in range(1, groups):
                block = out.at[v, :, (d + k) % groups, :, :, cols]
                last.append(send(block, block, p.at(v=1 - v)))
        else:
            block = out.at[v, 1 - u, :, :, :, cols]
            last.append(send(block, block, p.at(v=1 - v)))
    wait_all(last)
    for copy in every:
        copy.wait_send()
    yield None


def add_to(dst, terms, lead):
    total = 1
    for n in lead:
        total *= n

    def step(i, carry):
        index, rest = [], i
        for n in reversed(lead):
            index.insert(0, rest % n)
            rest = rest // n
        at = tuple(index) + (slice(None), slice(None))
        acc = dst[at].astype(jnp.float32)
        for term in terms:
            acc = acc + term[at].astype(jnp.float32)
        dst[at] = acc.astype(dst.dtype)
        return carry

    lax.fori_loop(0, total, step, 0)


def scatter_steps(p, sender, every, buf, landing, out, cols, u_first):
    groups, hi = p.groups, p.hi
    d, z, u, v = p.d, p.z, p.u, p.v
    r1, ru, rd, r4 = landing

    def send(src, dst, peer):
        copy = sender.start(src, dst, peer)
        every.append(copy)
        return copy

    going = [send(buf.at[1 - v, :, :, :, :, cols], r1, p.at(v=1 - v))]
    yield None
    wait_all(going)
    mine = buf.at[v, :, :, :, :, cols]
    add_to(mine, [r1], (2, groups, hi))
    if u_first:
        going = [
            send(buf.at[v, 1 - u, :, :, :, cols], ru, p.at(u=1 - u))
        ]
    else:
        going = [
            send(
                buf.at[v, :, (d + k) % groups, :, :, cols],
                rd.at[k - 1],
                p.at(d=(d + k) % groups),
            )
            for k in range(1, groups)
        ]
    yield None
    wait_all(going)
    if u_first:
        add_to(buf.at[v, u, :, :, :, cols], [ru], (groups, hi))
        going = [
            send(
                buf.at[v, u, (d + k) % groups, :, :, cols],
                rd.at[k - 1, 0],
                p.at(d=(d + k) % groups),
            )
            for k in range(1, groups)
        ]
    else:
        terms = [rd.at[k - 1] for k in range(1, groups)]
        add_to(buf.at[v, :, d, :, :, cols], terms, (2, hi))
        going = [send(buf.at[v, 1 - u, d, :, :, cols], ru.at[0], p.at(u=1 - u))]
    yield None
    wait_all(going)
    if u_first:
        terms = [rd.at[k - 1, 0] for k in range(1, groups)]
    else:
        terms = [ru.at[0]]
    add_to(buf.at[v, u, d, :, :, cols], terms, (hi,))
    going = [
        send(buf.at[v, u, d, (z + k) % hi, :, cols], r4.at[k - 1], p.at(z=(z + k) % hi))
        for k in range(1, hi)
    ]
    yield None
    wait_all(going)
    acc = buf[v, u, d, z, :, cols].astype(jnp.float32)
    for k in range(1, hi):
        acc = acc + r4[k - 1].astype(jnp.float32)
    out[:, cols] = acc.astype(out.dtype)
    yield None


def dot(left, right, dims):
    return lax.dot_general(left, right, (dims, ((), ())), preferred_element_type=jnp.float32)


def layer_kernel(groups, hi, *refs):
    x_ref, m_ref, gate_hbm, up_hbm, down_hbm = refs[0:5]
    out_ref, inner_ref, z_ref, low_ref, upper_ref, hid_ref = refs[5:11]
    gate_w, up_w, down_w, buf, mbuf, inner_s = refs[11:17]
    landing = [refs[17 + 4 * c : 21 + 4 * c] for c in range(CHUNKS + 1)]
    send_sem, recv_sem, local = refs[21 + 4 * CHUNKS :]
    p = Place(groups, hi)
    d, z, u, v = p.d, p.z, p.u, p.v
    width = x_ref.shape[1]
    hidden_dim = gate_w.shape[0]
    rows = z_ref.shape[0]
    loads = []
    for i, (src, dst) in enumerate(((gate_hbm, gate_w), (up_hbm, up_w), (down_hbm, down_w))):
        copy = pltpu.make_async_copy(src, dst, local.at[i])
        copy.start()
        loads.append(copy)
    own = []
    for i, (src, dst) in enumerate(((x_ref, buf), (m_ref, mbuf))):
        copy = pltpu.make_async_copy(src, dst.at[v, u, d, z], local.at[3 + i])
        copy.start()
        own.append(copy)
    greet(p)
    sender = Sender(send_sem, recv_sem)
    span = width // CHUNKS
    cuts = [(slice(c * span, (c + 1) * span), c % 2 == 1) for c in range(CHUNKS)]
    sources = [(x_ref, buf, cols, order) for cols, order in cuts]
    sources.append((m_ref, mbuf, slice(0, LANES), False))
    moves = gather(p, sender, sources)
    next(moves)
    for copy in own:
        copy.wait()
    next(moves)

    def place_of(shard):
        rest = shard // hi
        return (rest // (2 * groups), (rest // groups) % 2, rest % groups, shard % hi)

    def pack(i, carry):
        both = [buf[place_of(2 * i + j)].astype(jnp.float32) for j in range(2)]
        at = pl.ds(pl.multiple_of(i * 2 * UNIT, 2 * UNIT), 2 * UNIT)
        z_ref[at, :] = jnp.concatenate(both, axis=0).astype(jnp.bfloat16)
        return carry

    lax.fori_loop(0, rows // (2 * UNIT), pack, 0)
    for copy in loads:
        copy.wait()

    me = lax.axis_index("expert")
    block = min(rows, 256)
    units = block // UNIT
    tile = 256 if hidden_dim % 256 == 0 else hidden_dim
    lane = lax.broadcasted_iota(jnp.int32, (1, LANES), 1)

    def forward(i, carry):
        at = pl.ds(pl.multiple_of(i * block, block), block)
        planes = [mbuf[place_of(i * units + j)] for j in range(units)]
        dense = jnp.concatenate(planes, axis=0)
        gate = jnp.sum(jnp.where(lane == me, dense, 0.0), axis=1, keepdims=True)
        inner_s[...] = jnp.zeros_like(inner_s)

        def hidden_tile(f, c):
            if tile == hidden_dim:
                fs = slice(0, hidden_dim)
            else:
                fs = pl.ds(pl.multiple_of(f * tile, tile), tile)
            pre_gate = dot(z_ref[at, :], gate_w[fs, :], ((1,), (1,)))
            pre_up = dot(z_ref[at, :], up_w[fs, :], ((1,), (1,)))
            raw = dot(z_ref[at, :], down_w[fs, :], ((1,), (1,)))
            raw = pltpu.roll(raw, block - UNIT // 2, 0)
            squash = 1.0 / (1.0 + jnp.exp(-pre_gate))
            active = pre_gate * squash
            slope = squash * (1.0 + pre_gate * (1.0 - squash))
            hidden = active * pre_up
            inner_s[:, 0:1] += jnp.sum(hidden * raw, axis=1, keepdims=True)
            hidden = gate * hidden
            d_hidden = gate * raw
            d_upper = d_hidden * active
            d_lower = d_hidden * pre_up * slope
            half = UNIT // 2
            hid_ref[at, fs] = hidden.astype(jnp.bfloat16)
            low_ref[at, fs] = pltpu.roll(d_lower, half, 0).astype(jnp.bfloat16)
            upper_ref[at, fs] = pltpu.roll(d_upper, half, 0).astype(jnp.bfloat16)
            return c

        lax.fori_loop(0, hidden_dim // tile, hidden_tile, 0)
        part = jnp.where(lane == me, inner_s[:, 0:1], 0.0)
        for j in range(units):
            mbuf[place_of(i * units + j)] = part[j * UNIT : (j + 1) * UNIT]
        return carry

    lax.fori_loop(0, rows // block, forward, 0)

    every = []
    lines = [
        scatter_steps(p, sender, every, mbuf, landing[CHUNKS], inner_ref, slice(0, LANES), True)
    ]
    step = 256

    def backward(base):
        def one(n, carry):
            i, n = n // (span // step), n % (span // step)
            at = pl.ds(pl.multiple_of(i * block, block), block)
            cs = pl.ds(pl.multiple_of(base + n * step, step), step)
            acc = dot(hid_ref[at, :], down_w[:, cs], ((1,), (0,)))
            acc = acc + dot(low_ref[at, :], gate_w[:, cs], ((1,), (0,)))
            acc = acc + dot(upper_ref[at, :], up_w[:, cs], ((1,), (0,)))
            for j in range(units):
                a, b, c, e = place_of(i * units + j)
                buf[a, b, c, e, :, cs] = acc[j * UNIT : (j + 1) * UNIT].astype(jnp.bfloat16)
            return carry

        lax.fori_loop(0, (rows // block) * (span // step), one, 0)

    next(lines[0])
    for t in range(CHUNKS + 4):
        if t < CHUNKS:
            cols, order = cuts[t]
            backward(t * span)
            fresh = scatter_steps(p, sender, every, buf, landing[t], out_ref, cols, order)
            lines.append(fresh)
            next(fresh)
        for line in lines[: t + 1]:
            next(line, None)
    for copy in every:
        copy.wait_send()


def layer(groups, hi, x, m, gate_local, up_local, down_local):
    lead = (2, 2, groups, hi)
    rows = 4 * groups * hi * UNIT
    hidden_dim, width = gate_local.shape
    half = jax.ShapeDtypeStruct((rows, hidden_dim), jnp.bfloat16)

    def landing(cols, dtype, u_first):
        return [
            pltpu.VMEM((2, groups, hi, UNIT, cols), dtype),
            pltpu.VMEM((groups if u_first else 1, hi, UNIT, cols), dtype),
            pltpu.VMEM((groups - 1, 1 if u_first else 2, hi, UNIT, cols), dtype),
            pltpu.VMEM((hi - 1, UNIT, cols), dtype),
        ]

    moved = CHUNKS + 1
    copies = moved * 2 * (hi - 1 + groups - 1 + 1 + 2 * groups + 4)
    vmem = pl.BlockSpec(memory_space=pltpu.VMEM)
    weight = pltpu.VMEM((hidden_dim, width), jnp.bfloat16)
    return pl.pallas_call(
        functools.partial(layer_kernel, groups, hi),
        out_shape=[
            jax.ShapeDtypeStruct((UNIT, width), jnp.bfloat16),
            jax.ShapeDtypeStruct((UNIT, LANES), jnp.float32),
            jax.ShapeDtypeStruct((rows, width), jnp.bfloat16),
            half,
            half,
            half,
        ],
        in_specs=[vmem] * 2 + [pl.BlockSpec(memory_space=pl.ANY)] * 3,
        out_specs=[vmem] * 6,
        scratch_shapes=[weight] * 3
        + [
            pltpu.VMEM(lead + (UNIT, width), jnp.bfloat16),
            pltpu.VMEM(lead + (UNIT, LANES), jnp.float32),
        ]
        + [pltpu.VMEM((min(rows, 256), LANES), jnp.float32)]
        + sum([landing(width // CHUNKS, jnp.bfloat16, c % 2 == 1) for c in range(CHUNKS)], [])
        + landing(LANES, jnp.float32, True)
        + [
            pltpu.SemaphoreType.DMA((copies,)),
            pltpu.SemaphoreType.DMA((copies,)),
            pltpu.SemaphoreType.DMA((5,)),
        ],
        compiler_params=pltpu.CompilerParams(
            collective_id=0, has_side_effects=True, vmem_limit_bytes=VMEM_BYTES
        ),
        name="layer",
    )(x, m, gate_local, up_local, down_local)


def grad_kernel(z_ref, low_ref, upper_ref, hid_ref, gate_out, up_out, down_out, turned):
    @pl.when(pl.program_id(0) == 0)
    def _():
        rows, half = low_ref.shape[0], UNIT // 2
        shifts = (rows - half, rows - half, half)
        for i, ref in enumerate((low_ref, upper_ref, hid_ref)):
            moved = pltpu.roll(ref[...].astype(jnp.float32), shifts[i], 0)
            turned[i] = moved.astype(jnp.bfloat16).T

    for i, out in enumerate((gate_out, up_out, down_out)):
        out[0] = dot(turned[i], z_ref[...], ((1,), (0,))).astype(jnp.bfloat16)


def weight_grads(z_rows, low, upper, hid):
    rows, width = z_rows.shape
    hidden_dim = low.shape[1]
    tile = 512
    whole = pl.BlockSpec((rows, hidden_dim), lambda n: (0, 0))
    out = pl.BlockSpec((1, hidden_dim, tile), lambda n: (0, 0, n))
    return pl.pallas_call(
        grad_kernel,
        grid=(width // tile,),
        out_shape=[jax.ShapeDtypeStruct((1, hidden_dim, width), jnp.bfloat16)] * 3,
        in_specs=[pl.BlockSpec((rows, tile), lambda n: (0, n)), whole, whole, whole],
        out_specs=[out] * 3,
        scratch_shapes=[pltpu.VMEM((3, hidden_dim, rows), jnp.bfloat16)],
        compiler_params=pltpu.CompilerParams(vmem_limit_bytes=VMEM_BYTES // 2),
        name="weight_grads",
    )(z_rows, low, upper, hid)


def body(tokens, grad_output, routes, gate_weights, gate_proj, up_proj, down_proj):
    experts = lax.axis_size("expert")
    groups = lax.axis_size("dp")
    hi = experts // 4
    token_count = tokens.shape[0]
    lanes = jnp.arange(LANES, dtype=jnp.int32)
    chosen = routes[:, :, None] == lanes[None, None, :]
    dense = jnp.sum(jnp.where(chosen, gate_weights[:, :, None], 0.0), axis=1)
    both = jnp.concatenate([tokens, grad_output], axis=0)
    dense = jnp.concatenate([dense, jnp.zeros_like(dense)], axis=0)
    sums, inner, z_rows, low, upper, hid = layer(
        groups, hi, both, dense, gate_proj[0], up_proj[0], down_proj[0]
    )
    grads = weight_grads(z_rows, low, upper, hid)
    inner = inner[:token_count]
    grad_gates = jnp.sum(jnp.where(chosen, inner[:, None, :], 0.0), axis=2)
    return (sums[:token_count], sums[token_count:], grad_gates, *grads)


def solution(mesh):
    row = P(("dp", "expert"), None)
    weight = P("expert", "dp", None)
    return jax.shard_map(
        body,
        mesh=mesh,
        in_specs=(row,) * 4 + (weight,) * 3,
        out_specs=(row,) * 3 + (weight,) * 3,
        check_vma=False,
    )
```

```python
import functools

import jax
import jax.numpy as jnp
from jax import lax
from jax.experimental import pallas as pl
from jax.experimental.pallas import tpu as pltpu
from jax.sharding import PartitionSpec as P

MESH = pl.DeviceIdType.MESH
LANES = 128
UNIT = 8
CHUNKS = 4
PULLS = 4
VMEM_BYTES = 62 * 1024 * 1024


class Place:
    def __init__(self, groups, hi):
        self.groups, self.hi = groups, hi
        self.d = lax.axis_index("dp")
        e = lax.axis_index("expert")
        self.z, self.u, self.v = e // 4, (e // 2) % 2, e % 2

    def at(self, d=None, z=None, u=None, v=None):
        d = self.d if d is None else d
        z = self.z if z is None else z
        u = self.u if u is None else u
        v = self.v if v is None else v
        return (d, (z * 2 + u) * 2 + v)

    def peers(self):
        found = [self.at(z=(self.z + k) % self.hi) for k in range(1, self.hi)]
        found += [self.at(d=(self.d + k) % self.groups) for k in range(1, self.groups)]
        return found + [self.at(u=1 - self.u), self.at(v=1 - self.v)]


def greet(place):
    barrier = pltpu.get_barrier_semaphore()
    peers = place.peers()
    for peer in peers:
        pl.semaphore_signal(barrier, inc=1, device_id=peer, device_id_type=MESH)
    pl.semaphore_wait(barrier, len(peers))


class Sender:
    def __init__(self, send, recv):
        self.send, self.recv, self.used = send, recv, 0

    def start(self, src, dst, peer):
        slot = self.used
        self.used += 1
        copy = pltpu.make_async_remote_copy(
            src_ref=src,
            dst_ref=dst,
            send_sem=self.send.at[slot],
            recv_sem=self.recv.at[slot],
            device_id=peer,
            device_id_type=MESH,
        )
        copy.start()
        return copy


def wait_all(copies):
    for copy in copies:
        copy.wait_recv()


def gather(p, sender, sources):
    groups, hi = p.groups, p.hi
    d, z, u, v = p.d, p.z, p.u, p.v
    every = []

    def send(src, dst, peer):
        copy = sender.start(src, dst, peer)
        every.append(copy)
        return copy

    first = []
    for src, out, cols, _ in sources:
        first.append(
            [
                send(src.at[:, cols], out.at[v, u, d, z, :, cols], p.at(z=(z + k) % hi))
                for k in range(1, hi)
            ]
        )
    yield None
    second, third, last = [], [], []
    for i, (_, out, cols, u_first) in enumerate(sources):
        wait_all(first[i])
        block = out.at[v, u, d, :, :, cols]
        if u_first:
            second.append([send(block, block, p.at(u=1 - u))])
        else:
            second.append([send(block, block, p.at(d=(d + k) % groups)) for k in range(1, groups)])
        last.append(send(block, block, p.at(v=1 - v)))
    for i, (_, out, cols, u_first) in enumerate(sources):
        wait_all(second[i])
        if u_first:
            block = out.at[v, :, d, :, :, cols]
            third.append([send(block, block, p.at(d=(d + k) % groups)) for k in range(1, groups)])
            block = out.at[v, 1 - u, d, :, :, cols]
            last.append(send(block, block, p.at(v=1 - v)))
        else:
            block = out.at[v, u, :, :, :, cols]
            third.append([send(block, block, p.at(u=1 - u))])
            for k in range(1, groups):
                block = out.at[v, u, (d + k) % groups, :, :, cols]
                last.append(send(block, block, p.at(v=1 - v)))
    for i, (_, out, cols, u_first) in enumerate(sources):
        wait_all(third[i])
        if u_first:
            for k in range(1, groups):
                block = out.at[v, :, (d + k) % groups, :, :, cols]
                last.append(send(block, block, p.at(v=1 - v)))
        else:
            block = out.at[v, 1 - u, :, :, :, cols]
            last.append(send(block, block, p.at(v=1 - v)))
    wait_all(last)
    for copy in every:
        copy.wait_send()
    yield None


def add_to(dst, terms, lead):
    total = 1
    for n in lead[:-1]:
        total *= n

    def step(i, carry):
        index, rest = [], i
        for n in reversed(lead[:-1]):
            index.insert(0, rest % n)
            rest = rest // n
        for last in range(lead[-1]):
            at = tuple(index) + (last, slice(None), slice(None))
            acc = dst[at].astype(jnp.float32)
            for term in terms:
                acc = acc + term[at].astype(jnp.float32)
            dst[at] = acc.astype(dst.dtype)
        return carry

    if total == 1:
        step(0, 0)
    else:
        lax.fori_loop(0, total, step, 0)


def scatter_steps(p, sender, every, buf, landing, out, cols, u_first):
    groups, hi = p.groups, p.hi
    d, z, u, v = p.d, p.z, p.u, p.v
    r1, ru, rd, r4 = landing

    def send(src, dst, peer):
        copy = sender.start(src, dst, peer)
        every.append(copy)
        return copy

    going = [send(buf.at[1 - v, :, :, :, :, cols], r1, p.at(v=1 - v))]
    yield None
    wait_all(going)
    mine = buf.at[v, :, :, :, :, cols]
    add_to(mine, [r1], (2, groups, hi))
    if u_first:
        going = [
            send(buf.at[v, 1 - u, :, :, :, cols], ru, p.at(u=1 - u))
        ]
    else:
        going = [
            send(
                buf.at[v, :, (d + k) % groups, :, :, cols],
                rd.at[k - 1],
                p.at(d=(d + k) % groups),
            )
            for k in range(1, groups)
        ]
    yield None
    wait_all(going)
    if u_first:
        add_to(buf.at[v, u, :, :, :, cols], [ru], (groups, hi))
        going = [
            send(
                buf.at[v, u, (d + k) % groups, :, :, cols],
                rd.at[k - 1, 0],
                p.at(d=(d + k) % groups),
            )
            for k in range(1, groups)
        ]
    else:
        terms = [rd.at[k - 1] for k in range(1, groups)]
        add_to(buf.at[v, :, d, :, :, cols], terms, (2, hi))
        going = [send(buf.at[v, 1 - u, d, :, :, cols], ru.at[0], p.at(u=1 - u))]
    yield None
    wait_all(going)
    if u_first:
        terms = [rd.at[k - 1, 0] for k in range(1, groups)]
    else:
        terms = [ru.at[0]]
    add_to(buf.at[v, u, d, :, :, cols], terms, (hi,))
    going = [
        send(buf.at[v, u, d, (z + k) % hi, :, cols], r4.at[k - 1], p.at(z=(z + k) % hi))
        for k in range(1, hi)
    ]
    yield None
    wait_all(going)
    acc = buf[v, u, d, z, :, cols].astype(jnp.float32)
    for k in range(1, hi):
        acc = acc + r4[k - 1].astype(jnp.float32)
    out[:, cols] = acc.astype(out.dtype)
    yield None


def dot(left, right, dims):
    return lax.dot_general(left, right, (dims, ((), ())), preferred_element_type=jnp.float32)


def layer_kernel(groups, hi, *refs):
    tok_ref, dy_ref, m_ref, gate_hbm, up_hbm, down_hbm = refs[0:6]
    out_ref, inner_ref, z_ref, low_ref, upper_ref, hid_ref = refs[6:12]
    gate_w, up_w, down_w, buf, mbuf, inner_s, x_ref = refs[12:19]
    landing = [refs[19 + 4 * c : 23 + 4 * c] for c in range(CHUNKS + 1)]
    send_sem, recv_sem, local = refs[23 + 4 * CHUNKS :]
    p = Place(groups, hi)
    d, z, u, v = p.d, p.z, p.u, p.v
    width = tok_ref.shape[1]
    hidden_dim = gate_w.shape[0]
    rows = z_ref.shape[0]
    loads = []
    for i, (src, dst) in enumerate(((gate_hbm, gate_w), (up_hbm, up_w), (down_hbm, down_w))):
        copy = pltpu.make_async_copy(src, dst, local.at[i])
        copy.start()
        loads.append(copy)
    both = [ref[...].astype(jnp.float32) for ref in (tok_ref, dy_ref)]
    x_ref[...] = jnp.concatenate(both, axis=0).astype(jnp.bfloat16)
    own = []
    for i, (src, dst) in enumerate(((x_ref, buf), (m_ref, mbuf))):
        copy = pltpu.make_async_copy(src, dst.at[v, u, d, z], local.at[3 + i])
        copy.start()
        own.append(copy)
    greet(p)
    sender = Sender(send_sem, recv_sem)
    span = width // CHUNKS
    cuts = [(slice(c * span, (c + 1) * span), c % 2 == 1) for c in range(CHUNKS)]
    pull = width // PULLS
    sources = [
        (x_ref, buf, slice(c * pull, (c + 1) * pull), c % 2 == 1) for c in range(PULLS)
    ]
    sources.append((m_ref, mbuf, slice(0, LANES), False))
    moves = gather(p, sender, sources)
    next(moves)
    for copy in own:
        copy.wait()
    next(moves)

    def place_of(shard):
        rest = shard // hi
        return (rest // (2 * groups), (rest // groups) % 2, rest % groups, shard % hi)

    def pack(i, carry):
        both = [buf[place_of(2 * i + j)].astype(jnp.float32) for j in range(2)]
        at = pl.ds(pl.multiple_of(i * 2 * UNIT, 2 * UNIT), 2 * UNIT)
        z_ref[at, :] = jnp.concatenate(both, axis=0).astype(jnp.bfloat16)
        return carry

    lax.fori_loop(0, rows // (2 * UNIT), pack, 0)
    for copy in loads:
        copy.wait()

    me = lax.axis_index("expert")
    block = min(rows, 256)
    units = block // UNIT
    tile = 256 if hidden_dim % 256 == 0 else hidden_dim
    lane = lax.broadcasted_iota(jnp.int32, (1, LANES), 1)

    def forward(i, carry):
        at = pl.ds(pl.multiple_of(i * block, block), block)
        planes = [mbuf[place_of(i * units + j)] for j in range(units)]
        dense = jnp.concatenate(planes, axis=0)
        gate = jnp.sum(jnp.where(lane == me, dense, 0.0), axis=1, keepdims=True)
        inner_s[...] = jnp.zeros_like(inner_s)

        def hidden_tile(f, c):
            if tile == hidden_dim:
                fs = slice(0, hidden_dim)
            else:
                fs = pl.ds(pl.multiple_of(f * tile, tile), tile)
            pre_gate = dot(z_ref[at, :], gate_w[fs, :], ((1,), (1,)))
            pre_up = dot(z_ref[at, :], up_w[fs, :], ((1,), (1,)))
            raw = dot(z_ref[at, :], down_w[fs, :], ((1,), (1,)))
            raw = pltpu.roll(raw, block - UNIT // 2, 0)
            squash = 1.0 / (1.0 + jnp.exp(-pre_gate))
            active = pre_gate * squash
            slope = squash * (1.0 + pre_gate * (1.0 - squash))
            hidden = active * pre_up
            inner_s[:, 0:1] += jnp.sum(hidden * raw, axis=1, keepdims=True)
            hidden = gate * hidden
            d_hidden = gate * raw
            d_upper = d_hidden * active
            d_lower = d_hidden * pre_up * slope
            half = UNIT // 2
            hid_ref[at, fs] = hidden.astype(jnp.bfloat16)
            low_ref[at, fs] = pltpu.roll(d_lower, half, 0).astype(jnp.bfloat16)
            upper_ref[at, fs] = pltpu.roll(d_upper, half, 0).astype(jnp.bfloat16)
            return c

        lax.fori_loop(0, hidden_dim // tile, hidden_tile, 0)
        part = jnp.where(lane == me, inner_s[:, 0:1], 0.0)
        for j in range(units):
            mbuf[place_of(i * units + j)] = part[j * UNIT : (j + 1) * UNIT]
        return carry

    lax.fori_loop(0, rows // block, forward, 0)

    every = []
    lines = [
        scatter_steps(p, sender, every, mbuf, landing[CHUNKS], inner_ref, slice(0, LANES), True)
    ]
    step = 256

    def backward(base):
        def one(n, carry):
            i, n = n // (span // step), n % (span // step)
            at = pl.ds(pl.multiple_of(i * block, block), block)
            cs = pl.ds(pl.multiple_of(base + n * step, step), step)
            acc = dot(hid_ref[at, :], down_w[:, cs], ((1,), (0,)))
            acc = acc + dot(low_ref[at, :], gate_w[:, cs], ((1,), (0,)))
            acc = acc + dot(upper_ref[at, :], up_w[:, cs], ((1,), (0,)))
            for j in range(units):
                a, b, c, e = place_of(i * units + j)
                buf[a, b, c, e, :, cs] = acc[j * UNIT : (j + 1) * UNIT].astype(jnp.bfloat16)
            return carry

        lax.fori_loop(0, (rows // block) * (span // step), one, 0)

    next(lines[0])
    for t in range(CHUNKS + 4):
        if t < CHUNKS:
            cols, order = cuts[t]
            backward(t * span)
            fresh = scatter_steps(p, sender, every, buf, landing[t], out_ref, cols, order)
            lines.append(fresh)
            next(fresh)
        for line in lines[1 : t + 1] + lines[:1]:
            next(line, None)
    for copy in every:
        copy.wait_send()


def layer(groups, hi, x, dy, m, gate_local, up_local, down_local):
    lead = (2, 2, groups, hi)
    rows = 4 * groups * hi * UNIT
    hidden_dim, width = gate_local.shape
    half = jax.ShapeDtypeStruct((rows, hidden_dim), jnp.bfloat16)

    def landing(cols, dtype, u_first):
        return [
            pltpu.VMEM((2, groups, hi, UNIT, cols), dtype),
            pltpu.VMEM((groups if u_first else 1, hi, UNIT, cols), dtype),
            pltpu.VMEM((groups - 1, 1 if u_first else 2, hi, UNIT, cols), dtype),
            pltpu.VMEM((hi - 1, UNIT, cols), dtype),
        ]

    moved = max(CHUNKS, PULLS) + 1
    copies = moved * 2 * (hi - 1 + groups - 1 + 1 + 2 * groups + 4)
    vmem = pl.BlockSpec(memory_space=pltpu.VMEM)
    weight = pltpu.VMEM((hidden_dim, width), jnp.bfloat16)
    return pl.pallas_call(
        functools.partial(layer_kernel, groups, hi),
        out_shape=[
            jax.ShapeDtypeStruct((UNIT, width), jnp.bfloat16),
            jax.ShapeDtypeStruct((UNIT, LANES), jnp.float32),
            jax.ShapeDtypeStruct((rows, width), jnp.bfloat16),
            half,
            half,
            half,
        ],
        in_specs=[vmem] * 3 + [pl.BlockSpec(memory_space=pl.ANY)] * 3,
        out_specs=[vmem] * 6,
        scratch_shapes=[weight] * 3
        + [
            pltpu.VMEM(lead + (UNIT, width), jnp.bfloat16),
            pltpu.VMEM(lead + (UNIT, LANES), jnp.float32),
        ]
        + [pltpu.VMEM((min(rows, 256), LANES), jnp.float32)]
        + [pltpu.VMEM((UNIT, width), jnp.bfloat16)]
        + sum([landing(width // CHUNKS, jnp.bfloat16, c % 2 == 1) for c in range(CHUNKS)], [])
        + landing(LANES, jnp.float32, True)
        + [
            pltpu.SemaphoreType.DMA((copies,)),
            pltpu.SemaphoreType.DMA((copies,)),
            pltpu.SemaphoreType.DMA((5,)),
        ],
        compiler_params=pltpu.CompilerParams(
            collective_id=0, has_side_effects=True, vmem_limit_bytes=VMEM_BYTES
        ),
        name="layer",
    )(x, dy, m, gate_local, up_local, down_local)


def grad_kernel(z_ref, low_ref, upper_ref, hid_ref, gate_out, up_out, down_out, turned):
    @pl.when(pl.program_id(0) == 0)
    def _():
        rows, half = low_ref.shape[0], UNIT // 2
        shifts = (rows - half, rows - half, half)
        for i, ref in enumerate((low_ref, upper_ref, hid_ref)):
            moved = pltpu.roll(ref[...].astype(jnp.float32), shifts[i], 0)
            turned[i] = moved.astype(jnp.bfloat16).T

    for i, out in enumerate((gate_out, up_out, down_out)):
        out[0] = dot(turned[i], z_ref[...], ((1,), (0,))).astype(jnp.bfloat16)


def weight_grads(z_rows, low, upper, hid):
    rows, width = z_rows.shape
    hidden_dim = low.shape[1]
    tile = 512
    whole = pl.BlockSpec((rows, hidden_dim), lambda n: (0, 0))
    out = pl.BlockSpec((1, hidden_dim, tile), lambda n: (0, 0, n))
    return pl.pallas_call(
        grad_kernel,
        grid=(width // tile,),
        out_shape=[jax.ShapeDtypeStruct((1, hidden_dim, width), jnp.bfloat16)] * 3,
        in_specs=[pl.BlockSpec((rows, tile), lambda n: (0, n)), whole, whole, whole],
        out_specs=[out] * 3,
        scratch_shapes=[pltpu.VMEM((3, hidden_dim, rows), jnp.bfloat16)],
        compiler_params=pltpu.CompilerParams(vmem_limit_bytes=VMEM_BYTES),
        name="weight_grads",
    )(z_rows, low, upper, hid)


def body(tokens, grad_output, routes, gate_weights, gate_proj, up_proj, down_proj):
    experts = lax.axis_size("expert")
    groups = lax.axis_size("dp")
    hi = experts // 4
    token_count = tokens.shape[0]
    lanes = jnp.arange(LANES, dtype=jnp.int32)
    chosen = routes[:, :, None] == lanes[None, None, :]
    dense = jnp.sum(jnp.where(chosen, gate_weights[:, :, None], 0.0), axis=1)
    dense = jnp.concatenate([dense, jnp.zeros_like(dense)], axis=0)
    sums, inner, z_rows, low, upper, hid = layer(
        groups, hi, tokens, grad_output, dense, gate_proj[0], up_proj[0], down_proj[0]
    )
    grads = weight_grads(z_rows, low, upper, hid)
    inner = inner[:token_count]
    grad_gates = jnp.sum(jnp.where(chosen, inner[:, None, :], 0.0), axis=2)
    return (sums[:token_count], sums[token_count:], grad_gates, *grads)


def solution(mesh):
    row = P(("dp", "expert"), None)
    weight = P("expert", "dp", None)
    return jax.shard_map(
        body,
        mesh=mesh,
        in_specs=(row,) * 4 + (weight,) * 3,
        out_specs=(row,) * 3 + (weight,) * 3,
        check_vma=False,
    )
```

```python
import functools

import jax
import jax.numpy as jnp
from jax import lax
from jax.experimental import pallas as pl
from jax.experimental.pallas import tpu as pltpu
from jax.sharding import PartitionSpec as P

MESH = pl.DeviceIdType.MESH
LANES = 128
UNIT = 8
CHUNKS = 4
PULLS = 4
VMEM_BYTES = 62 * 1024 * 1024


class Place:
    def __init__(self, groups, hi):
        self.groups, self.hi = groups, hi
        self.d = lax.axis_index("dp")
        e = lax.axis_index("expert")
        self.z, self.u, self.v = e // 4, (e // 2) % 2, e % 2

    def at(self, d=None, z=None, u=None, v=None):
        d = self.d if d is None else d
        z = self.z if z is None else z
        u = self.u if u is None else u
        v = self.v if v is None else v
        return (d, (z * 2 + u) * 2 + v)

    def peers(self):
        found = [self.at(z=(self.z + k) % self.hi) for k in range(1, self.hi)]
        found += [self.at(d=(self.d + k) % self.groups) for k in range(1, self.groups)]
        return found + [self.at(u=1 - self.u), self.at(v=1 - self.v)]


def greet(place):
    barrier = pltpu.get_barrier_semaphore()
    peers = place.peers()
    for peer in peers:
        pl.semaphore_signal(barrier, inc=1, device_id=peer, device_id_type=MESH)
    pl.semaphore_wait(barrier, len(peers))


class Sender:
    def __init__(self, send, recv):
        self.send, self.recv, self.used = send, recv, 0

    def start(self, src, dst, peer):
        slot = self.used
        self.used += 1
        copy = pltpu.make_async_remote_copy(
            src_ref=src,
            dst_ref=dst,
            send_sem=self.send.at[slot],
            recv_sem=self.recv.at[slot],
            device_id=peer,
            device_id_type=MESH,
        )
        copy.start()
        return copy


def wait_all(copies):
    for copy in copies:
        copy.wait_recv()


def gather(p, sender, sources):
    groups, hi = p.groups, p.hi
    d, z, u, v = p.d, p.z, p.u, p.v
    every = []

    def send(src, dst, peer):
        copy = sender.start(src, dst, peer)
        every.append(copy)
        return copy

    first = []
    for src, out, cols, _ in sources:
        first.append(
            [
                send(src.at[:, cols], out.at[v, u, d, z, :, cols], p.at(z=(z + k) % hi))
                for k in range(1, hi)
            ]
        )
    yield None
    second, third, last = [], [], []
    for i, (_, out, cols, u_first) in enumerate(sources):
        wait_all(first[i])
        block = out.at[v, u, d, :, :, cols]
        if u_first:
            second.append([send(block, block, p.at(u=1 - u))])
        else:
            second.append([send(block, block, p.at(d=(d + k) % groups)) for k in range(1, groups)])
        last.append(send(block, block, p.at(v=1 - v)))
    for i, (_, out, cols, u_first) in enumerate(sources):
        wait_all(second[i])
        if u_first:
            block = out.at[v, :, d, :, :, cols]
            third.append([send(block, block, p.at(d=(d + k) % groups)) for k in range(1, groups)])
            block = out.at[v, 1 - u, d, :, :, cols]
            last.append(send(block, block, p.at(v=1 - v)))
        else:
            block = out.at[v, u, :, :, :, cols]
            third.append([send(block, block, p.at(u=1 - u))])
            for k in range(1, groups):
                block = out.at[v, u, (d + k) % groups, :, :, cols]
                last.append(send(block, block, p.at(v=1 - v)))
    for i, (_, out, cols, u_first) in enumerate(sources):
        wait_all(third[i])
        if u_first:
            for k in range(1, groups):
                block = out.at[v, :, (d + k) % groups, :, :, cols]
                last.append(send(block, block, p.at(v=1 - v)))
        else:
            block = out.at[v, 1 - u, :, :, :, cols]
            last.append(send(block, block, p.at(v=1 - v)))
    wait_all(last)
    for copy in every:
        copy.wait_send()
    yield None


def add_to(dst, terms, lead):
    total = 1
    for n in lead[:-1]:
        total *= n

    def step(i, carry):
        index, rest = [], i
        for n in reversed(lead[:-1]):
            index.insert(0, rest % n)
            rest = rest // n
        for last in range(lead[-1]):
            at = tuple(index) + (last, slice(None), slice(None))
            acc = dst[at].astype(jnp.float32)
            for term in terms:
                acc = acc + term[at].astype(jnp.float32)
            dst[at] = acc.astype(dst.dtype)
        return carry

    if total == 1:
        step(0, 0)
    else:
        lax.fori_loop(0, total, step, 0)


def scatter_steps(p, sender, every, buf, landing, out, cols, u_first):
    groups, hi = p.groups, p.hi
    d, z, u, v = p.d, p.z, p.u, p.v
    r1, ru, rd, r4 = landing

    def send(src, dst, peer):
        copy = sender.start(src, dst, peer)
        every.append(copy)
        return copy

    going = [send(buf.at[1 - v, :, :, :, :, cols], r1, p.at(v=1 - v))]
    yield None
    wait_all(going)
    mine = buf.at[v, :, :, :, :, cols]
    add_to(mine, [r1], (2, groups, hi))
    if u_first:
        going = [
            send(buf.at[v, 1 - u, :, :, :, cols], ru, p.at(u=1 - u))
        ]
    else:
        going = [
            send(
                buf.at[v, :, (d + k) % groups, :, :, cols],
                rd.at[k - 1],
                p.at(d=(d + k) % groups),
            )
            for k in range(1, groups)
        ]
    yield None
    wait_all(going)
    if u_first:
        add_to(buf.at[v, u, :, :, :, cols], [ru], (groups, hi))
        going = [
            send(
                buf.at[v, u, (d + k) % groups, :, :, cols],
                rd.at[k - 1, 0],
                p.at(d=(d + k) % groups),
            )
            for k in range(1, groups)
        ]
    else:
        terms = [rd.at[k - 1] for k in range(1, groups)]
        add_to(buf.at[v, :, d, :, :, cols], terms, (2, hi))
        going = [send(buf.at[v, 1 - u, d, :, :, cols], ru.at[0], p.at(u=1 - u))]
    yield None
    wait_all(going)
    if u_first:
        terms = [rd.at[k - 1, 0] for k in range(1, groups)]
    else:
        terms = [ru.at[0]]
    add_to(buf.at[v, u, d, :, :, cols], terms, (hi,))
    going = [
        send(buf.at[v, u, d, (z + k) % hi, :, cols], r4.at[k - 1], p.at(z=(z + k) % hi))
        for k in range(1, hi)
    ]
    yield None
    wait_all(going)
    acc = buf[v, u, d, z, :, cols].astype(jnp.float32)
    for k in range(1, hi):
        acc = acc + r4[k - 1].astype(jnp.float32)
    out[:, cols] = acc.astype(out.dtype)
    yield None


def dot(left, right, dims):
    return lax.dot_general(left, right, (dims, ((), ())), preferred_element_type=jnp.float32)


def layer_kernel(groups, hi, *refs):
    tok_ref, dy_ref, m_ref, gate_hbm, up_hbm, down_hbm = refs[0:6]
    out_ref, inner_ref, z_ref, low_ref, upper_ref, hid_ref = refs[6:12]
    gate_w, up_w, down_w, buf, mbuf, inner_s, x_ref = refs[12:19]
    landing = [refs[19 + 4 * c : 23 + 4 * c] for c in range(CHUNKS + 1)]
    send_sem, recv_sem, local = refs[23 + 4 * CHUNKS :]
    p = Place(groups, hi)
    d, z, u, v = p.d, p.z, p.u, p.v
    width = tok_ref.shape[1]
    hidden_dim = gate_w.shape[0]
    rows = z_ref.shape[0]
    loads = []
    for i, (src, dst) in enumerate(((gate_hbm, gate_w), (up_hbm, up_w), (down_hbm, down_w))):
        copy = pltpu.make_async_copy(src, dst, local.at[i])
        copy.start()
        loads.append(copy)
    both = [ref[...].astype(jnp.float32) for ref in (tok_ref, dy_ref)]
    x_ref[...] = jnp.concatenate(both, axis=0).astype(jnp.bfloat16)
    own = []
    for i, (src, dst) in enumerate(((x_ref, buf), (m_ref, mbuf))):
        copy = pltpu.make_async_copy(src, dst.at[v, u, d, z], local.at[3 + i])
        copy.start()
        own.append(copy)
    greet(p)
    sender = Sender(send_sem, recv_sem)
    span = width // CHUNKS
    cuts = [(slice(c * span, (c + 1) * span), c % 2 == 1) for c in range(CHUNKS)]
    pull = width // PULLS
    sources = [
        (x_ref, buf, slice(c * pull, (c + 1) * pull), c % 2 == 1) for c in range(PULLS)
    ]
    sources.append((m_ref, mbuf, slice(0, LANES), False))
    moves = gather(p, sender, sources)
    next(moves)
    for copy in own:
        copy.wait()
    next(moves)

    def place_of(shard):
        rest = shard // hi
        return (rest // (2 * groups), (rest // groups) % 2, rest % groups, shard % hi)

    def pack(i, carry):
        both = [buf[place_of(2 * i + j)].astype(jnp.float32) for j in range(2)]
        at = pl.ds(pl.multiple_of(i * 2 * UNIT, 2 * UNIT), 2 * UNIT)
        z_ref[at, :] = jnp.concatenate(both, axis=0).astype(jnp.bfloat16)
        return carry

    lax.fori_loop(0, rows // (2 * UNIT), pack, 0)
    for copy in loads:
        copy.wait()

    me = lax.axis_index("expert")
    block = min(rows, 256)
    units = block // UNIT
    tile = 256 if hidden_dim % 256 == 0 else hidden_dim
    lane = lax.broadcasted_iota(jnp.int32, (1, LANES), 1)

    def forward(i, carry):
        at = pl.ds(pl.multiple_of(i * block, block), block)
        planes = [mbuf[place_of(i * units + j)] for j in range(units)]
        dense = jnp.concatenate(planes, axis=0)
        gate = jnp.sum(jnp.where(lane == me, dense, 0.0), axis=1, keepdims=True)
        inner_s[...] = jnp.zeros_like(inner_s)

        def hidden_tile(f, c):
            if tile == hidden_dim:
                fs = slice(0, hidden_dim)
            else:
                fs = pl.ds(pl.multiple_of(f * tile, tile), tile)
            pre_gate = dot(z_ref[at, :], gate_w[fs, :], ((1,), (1,)))
            pre_up = dot(z_ref[at, :], up_w[fs, :], ((1,), (1,)))
            raw = dot(z_ref[at, :], down_w[fs, :], ((1,), (1,)))
            raw = pltpu.roll(raw, block - UNIT // 2, 0)
            squash = 1.0 / (1.0 + jnp.exp(-pre_gate))
            active = pre_gate * squash
            slope = squash * (1.0 + pre_gate * (1.0 - squash))
            hidden = active * pre_up
            inner_s[:, 0:1] += jnp.sum(hidden * raw, axis=1, keepdims=True)
            hidden = gate * hidden
            d_hidden = gate * raw
            d_upper = d_hidden * active
            d_lower = d_hidden * pre_up * slope
            half = UNIT // 2
            hid_ref[at, fs] = hidden.astype(jnp.bfloat16)
            low_ref[at, fs] = pltpu.roll(d_lower, half, 0).astype(jnp.bfloat16)
            upper_ref[at, fs] = pltpu.roll(d_upper, half, 0).astype(jnp.bfloat16)
            return c

        lax.fori_loop(0, hidden_dim // tile, hidden_tile, 0)
        part = jnp.where(lane == me, inner_s[:, 0:1], 0.0)
        for j in range(units):
            mbuf[place_of(i * units + j)] = part[j * UNIT : (j + 1) * UNIT]
        return carry

    lax.fori_loop(0, rows // block, forward, 0)

    every = []
    lines = [
        scatter_steps(p, sender, every, mbuf, landing[CHUNKS], inner_ref, slice(0, LANES), True)
    ]
    step = 256

    def backward(base):
        def one(n, carry):
            i, n = n // (span // step), n % (span // step)
            at = pl.ds(pl.multiple_of(i * block, block), block)
            cs = pl.ds(pl.multiple_of(base + n * step, step), step)
            acc = dot(hid_ref[at, :], down_w[:, cs], ((1,), (0,)))
            acc = acc + dot(low_ref[at, :], gate_w[:, cs], ((1,), (0,)))
            acc = acc + dot(upper_ref[at, :], up_w[:, cs], ((1,), (0,)))
            for j in range(units):
                a, b, c, e = place_of(i * units + j)
                buf[a, b, c, e, :, cs] = acc[j * UNIT : (j + 1) * UNIT].astype(jnp.bfloat16)
            return carry

        lax.fori_loop(0, (rows // block) * (span // step), one, 0)

    next(lines[0])
    for t in range(CHUNKS + 4):
        if t < CHUNKS:
            cols, order = cuts[t]
            backward(t * span)
            fresh = scatter_steps(p, sender, every, buf, landing[t], out_ref, cols, order)
            lines.append(fresh)
            next(fresh)
        for line in lines[1 : t + 1] + lines[:1]:
            next(line, None)
    for copy in every:
        copy.wait_send()


def layer(groups, hi, x, dy, m, gate_local, up_local, down_local):
    lead = (2, 2, groups, hi)
    rows = 4 * groups * hi * UNIT
    hidden_dim, width = gate_local.shape
    half = jax.ShapeDtypeStruct((rows, hidden_dim), jnp.bfloat16)

    def landing(cols, dtype, u_first):
        return [
            pltpu.VMEM((2, groups, hi, UNIT, cols), dtype),
            pltpu.VMEM((groups if u_first else 1, hi, UNIT, cols), dtype),
            pltpu.VMEM((groups - 1, 1 if u_first else 2, hi, UNIT, cols), dtype),
            pltpu.VMEM((hi - 1, UNIT, cols), dtype),
        ]

    moved = max(CHUNKS, PULLS) + 1
    copies = moved * 2 * (hi - 1 + groups - 1 + 1 + 2 * groups + 4)
    vmem = pl.BlockSpec(memory_space=pltpu.VMEM)
    weight = pltpu.VMEM((hidden_dim, width), jnp.bfloat16)
    return pl.pallas_call(
        functools.partial(layer_kernel, groups, hi),
        out_shape=[
            jax.ShapeDtypeStruct((UNIT, width), jnp.bfloat16),
            jax.ShapeDtypeStruct((UNIT, LANES), jnp.float32),
            jax.ShapeDtypeStruct((rows, width), jnp.bfloat16),
            half,
            half,
            half,
        ],
        in_specs=[vmem] * 3 + [pl.BlockSpec(memory_space=pl.ANY)] * 3,
        out_specs=[vmem] * 6,
        scratch_shapes=[weight] * 3
        + [
            pltpu.VMEM(lead + (UNIT, width), jnp.bfloat16),
            pltpu.VMEM(lead + (UNIT, LANES), jnp.float32),
        ]
        + [pltpu.VMEM((min(rows, 256), LANES), jnp.float32)]
        + [pltpu.VMEM((UNIT, width), jnp.bfloat16)]
        + sum([landing(width // CHUNKS, jnp.bfloat16, c % 2 == 1) for c in range(CHUNKS)], [])
        + landing(LANES, jnp.float32, True)
        + [
            pltpu.SemaphoreType.DMA((copies,)),
            pltpu.SemaphoreType.DMA((copies,)),
            pltpu.SemaphoreType.DMA((5,)),
        ],
        compiler_params=pltpu.CompilerParams(
            collective_id=0, has_side_effects=True, vmem_limit_bytes=VMEM_BYTES
        ),
        name="layer",
    )(x, dy, m, gate_local, up_local, down_local)


def grad_kernel(z_ref, low_ref, upper_ref, hid_ref, gate_out, up_out, down_out, turned):
    @pl.when(pl.program_id(0) == 0)
    def _():
        rows, half = low_ref.shape[0], UNIT // 2
        shifts = (rows - half, rows - half, half)
        for i, ref in enumerate((low_ref, upper_ref, hid_ref)):
            moved = pltpu.roll(ref[...].astype(jnp.float32), shifts[i], 0)
            turned[i] = moved.astype(jnp.bfloat16).T

    for i, out in enumerate((gate_out, up_out, down_out)):
        out[0] = dot(turned[i], z_ref[...], ((1,), (0,))).astype(jnp.bfloat16)


def weight_grads(z_rows, low, upper, hid):
    rows, width = z_rows.shape
    hidden_dim = low.shape[1]
    tile = 256
    whole = pl.BlockSpec((rows, hidden_dim), lambda n: (0, 0))
    out = pl.BlockSpec((1, hidden_dim, tile), lambda n: (0, 0, n))
    return pl.pallas_call(
        grad_kernel,
        grid=(width // tile,),
        out_shape=[jax.ShapeDtypeStruct((1, hidden_dim, width), jnp.bfloat16)] * 3,
        in_specs=[pl.BlockSpec((rows, tile), lambda n: (0, n)), whole, whole, whole],
        out_specs=[out] * 3,
        scratch_shapes=[pltpu.VMEM((3, hidden_dim, rows), jnp.bfloat16)],
        compiler_params=pltpu.CompilerParams(vmem_limit_bytes=VMEM_BYTES),
        name="weight_grads",
    )(z_rows, low, upper, hid)


def body(tokens, grad_output, routes, gate_weights, gate_proj, up_proj, down_proj):
    experts = lax.axis_size("expert")
    groups = lax.axis_size("dp")
    hi = experts // 4
    token_count = tokens.shape[0]
    lanes = jnp.arange(LANES, dtype=jnp.int32)
    chosen = routes[:, :, None] == lanes[None, None, :]
    dense = jnp.sum(jnp.where(chosen, gate_weights[:, :, None], 0.0), axis=1)
    dense = jnp.concatenate([dense, jnp.zeros_like(dense)], axis=0)
    sums, inner, z_rows, low, upper, hid = layer(
        groups, hi, tokens, grad_output, dense, gate_proj[0], up_proj[0], down_proj[0]
    )
    grads = weight_grads(z_rows, low, upper, hid)
    inner = inner[:token_count]
    grad_gates = jnp.sum(jnp.where(chosen, inner[:, None, :], 0.0), axis=2)
    return (sums[:token_count], sums[token_count:], grad_gates, *grads)


def solution(mesh):
    row = P(("dp", "expert"), None)
    weight = P("expert", "dp", None)
    return jax.shard_map(
        body,
        mesh=mesh,
        in_specs=(row,) * 4 + (weight,) * 3,
        out_specs=(row,) * 3 + (weight,) * 3,
        check_vma=False,
    )
```
